32 devices in a mesh: dom: 16 (over z, y, core), band: 2 (over x).
Axes of the slice: x: 2, y: 2, z: 4, core: 2. Of those that a mesh axis runs over, the one named last changes fastest.
Arguments:
- wavefunctions: float32 [32, 512, 1536], P('dom', None, 'band'), may hold values from -6 to 6
- cell_hamiltonian: float32 [32, 512, 512], P('dom'), as said below
- face_nodes: int32 [16, 2, 128], P('dom'), may hold values from 0 to 1023, as said below
Outputs:
- filtered: float32 [32, 512, 1536], P('dom', None, 'band')
- margin: float32 [1536, 1536], P('dom', 'band')
The draws below stay inside these ranges and needn't reach their ends.
Inputs may be any that keep to these rules, and one draw needn't show every extreme that they name: `face_nodes`: the 256 entries of one domain are all different. `cell_hamiltonian`: each cell's matrix is symmetric.
All inputs are finite; a program needn't handle non-finite values.
Results may differ from the reference program's by a relative error of at most 0.0001.
Values sent between devices are 32-bit elements; how exact they have to be, the bound alone decides.
A program may use at most 64 MiB of HBM per device.

```python
import jax
import jax.numpy as jnp
from jax import lax

NODES = 512
FACE = 128
BANDS = 1536
CELL_DEV = 2
DEGREE = 4
DOMAINS = 16
CELLS = 32


def draw_cell_hamiltonian(key, part):
    raw = jax.random.normal(jax.random.fold_in(key, 11), (CELLS, NODES, NODES), jnp.float32)
    sym = (raw + jnp.swapaxes(raw, 1, 2)) * (0.5 / (2.0 * NODES) ** 0.5)
    return sym


def draw_face_nodes(key, part):
    keys = jax.random.split(jax.random.fold_in(key, 23), DOMAINS)
    slots = CELL_DEV * NODES
    top = jnp.int32(slots - 1)

    def one_domain(sub, number):
        order = jax.random.permutation(sub, slots).astype(jnp.int32)
        where_top = jnp.argmax(order == top)
        first_value = order[0]
        swapped = order.at[where_top].set(first_value).at[0].set(top)
        chosen = jnp.where(number == 0, swapped, order)
        return chosen[:2 * FACE].reshape(2, FACE).astype(jnp.int32)
    return jax.vmap(one_domain)(keys, jnp.arange(DOMAINS, dtype=jnp.int32))


def shard_levels(rng, extent, cuts, smallest, high):
    level = 1.0
    for axis_at, parts in cuts:
        steps = jax.random.uniform(jax.random.fold_in(jax.random.fold_in(rng, 6), axis_at), (parts,), jnp.float32, smallest / len(cuts), high / len(cuts))
        level = level * jnp.repeat(jnp.exp(steps), extent[axis_at] // parts).reshape((-1,) + (1,) * (len(extent) - 1 - axis_at))
    return level


def scatter_about(rng, dims, spread, bound, cuts=(), held_as=jnp.bfloat16):
    level = shard_levels(rng, dims, cuts, -0.22, 0.18) if cuts else 1.0
    result = jax.random.normal(rng, dims, jnp.float32) * spread * level
    return jnp.minimum(jnp.maximum(result, -bound), bound).astype(held_as)


def setup_inputs(seed: int = 0) -> dict:
    key_of = jax.random.split(jax.random.key(seed), 4)
    return {
        "wavefunctions": scatter_about(key_of[0], (CELLS, NODES, BANDS), 1.0, 6.0, ((0, 16), (2, 2)), jnp.float32),
        "cell_hamiltonian": draw_cell_hamiltonian(jax.random.fold_in(key_of[3], 71), 0),
        "face_nodes": draw_face_nodes(jax.random.fold_in(key_of[3], 71), 0),
    }


def assemble(local, faces):
    rims = jax.vmap(lambda value, index: value[index])(local, faces)
    from_prev = jnp.roll(rims[:, 1], 1, axis=0)
    from_next = jnp.roll(rims[:, 0], -1, axis=0)

    def add_one(value, index, lower, upper):
        return value.at[index[0]].add(lower).at[index[1]].add(upper)

    return jax.vmap(add_one)(local, faces, from_prev, from_next)


def operate(field, cell_hamiltonian, face_nodes):
    local = jnp.einsum("cij,cjb->cib", cell_hamiltonian, field, precision=lax.Precision.HIGHEST)
    domains = face_nodes.shape[0]
    local = local.reshape(domains, -1, field.shape[-1])
    summed = assemble(local, face_nodes)
    return 0.5 * summed.reshape(field.shape)


def reference(wavefunctions, cell_hamiltonian, face_nodes):
    previous = wavefunctions
    current = operate(wavefunctions, cell_hamiltonian, face_nodes)
    for step in range(DEGREE - 1):
        following = 2.0 * operate(current, cell_hamiltonian, face_nodes) - previous
        previous = current
        current = following
    flat = current.reshape(-1, current.shape[-1])
    margin = lax.dot_general(flat, flat, (((0,), (0,)), ((), ())), precision=lax.Precision.HIGHEST, preferred_element_type=jnp.float32)
    margin = margin / float(CELL_DEV * NODES)
    return current, margin
```

```python
import jax
import jax.numpy as jnp
from jax import lax
from jax.sharding import PartitionSpec as P

NODES = 512
CELL_DEV = 2
DEGREE = 4
HIGH = lax.Precision.HIGH


def passed_along(value, axis, steps):
    count = lax.axis_size(axis)
    pairs = [(source, (source + steps) % count) for source in range(count)]
    return lax.ppermute(value, axis, pairs)


def local_step(field, ham):
    return lax.dot_general(
        ham, field, (((2,), (1,)), ((0,), (0,))), precision=HIGH, preferred_element_type=jnp.float32
    )


def on_device(wavefunctions, cell_hamiltonian, face_nodes):
    cells, nodes, width = wavefunctions.shape
    faces = face_nodes[0]
    slots = faces.reshape(-1)
    owner = slots // nodes
    rows = cell_hamiltonian.reshape(cells * nodes, nodes)[slots]
    mine = owner[None, :] == jnp.arange(cells)[:, None]
    rim_ham = jnp.where(mine[:, :, None], rows[None], 0.0)
    rim_ham = jnp.swapaxes(rim_ham, 0, 1).reshape(slots.shape[0], cells * nodes)
    spread = (jnp.arange(cells * nodes)[:, None] == slots[None, :]).astype(jnp.float32)

    def assembled(field):
        flat = field.reshape(cells * nodes, width)
        rims = jnp.dot(rim_ham, flat, precision=HIGH, preferred_element_type=jnp.float32)
        rims = rims.reshape(2, faces.shape[1], width)
        lower = passed_along(rims[1], "dom", 1)
        upper = passed_along(rims[0], "dom", -1)
        local = local_step(field, cell_hamiltonian)
        came = jnp.concatenate([lower, upper], axis=0)
        gained = jnp.dot(spread, came, precision=HIGH, preferred_element_type=jnp.float32)
        return local + gained.reshape(field.shape)

    previous = wavefunctions
    current = 0.5 * assembled(wavefunctions)
    for step in range(DEGREE - 1):
        following = assembled(current) - previous
        previous = current
        current = following
    flat = current.reshape(cells * nodes, width)
    other = passed_along(flat, "band", 1)

    def inner_block(left, right):
        return lax.dot_general(
            left, right, (((0,), (0,)), ((), ())), precision=HIGH, preferred_element_type=jnp.float32
        )

    own_tile = inner_block(flat, flat)
    cross_tile = inner_block(other, flat)
    first = lax.axis_index("band") == 0
    upper = jnp.where(first, own_tile, cross_tile)
    lower = jnp.where(first, cross_tile, own_tile)
    partial_rows = jnp.concatenate([upper, lower], axis=0)
    margin = lax.psum_scatter(partial_rows, "dom", scatter_dimension=0, tiled=True)
    margin = margin / float(CELL_DEV * NODES)
    return (current, margin)


def solution(mesh):
    return jax.shard_map(
        on_device,
        mesh=mesh,
        in_specs=(P("dom", None, "band"), P("dom", None, None), P("dom", None, None)),
        out_specs=(P("dom", None, "band"), P("dom", "band")),
        check_vma=False,
    )
```

```python
import functools

import jax
import jax.numpy as jnp
from jax import lax
from jax.experimental import pallas as pl
from jax.experimental.pallas import tpu as pltpu
from jax.sharding import PartitionSpec as P

NODES = 512
CELL_DEV = 2
DEGREE = 4
HIGH = lax.Precision.HIGH


def passed_along(value, axis, steps):
    count = lax.axis_size(axis)
    pairs = [(source, (source + steps) % count) for source in range(count)]
    return lax.ppermute(value, axis, pairs)


def local_step(field, ham):
    return lax.dot_general(
        ham, field, (((2,), (1,)), ((0,), (0,))), precision=HIGH, preferred_element_type=jnp.float32
    )


def by_bits(tile, blocks):
    bits = blocks.bit_length() - 1
    rows, width = tile.shape[0] // blocks, tile.shape[1]
    cut = tile.reshape((2,) * bits + (rows, width))
    order = tuple(reversed(range(bits))) + (bits, bits + 1)
    return jnp.transpose(cut, order).reshape(blocks, rows, width)


def halving_kernel(blocks, chunk, last, *refs):
    bits = blocks.bit_length() - 1
    refs = list(refs)
    tile = refs.pop(0)
    own = refs.pop(0) if last else None
    out = refs.pop(0)
    sums = [refs.pop(0) for _ in range(bits)]
    came = [refs.pop(0) for _ in range(bits)]
    if last:
        leaving, arrived = refs.pop(0), refs.pop(0)
    send_sem, recv_sem = refs
    chunks = tile.shape[2] // chunk
    steps = bits + 1 if last else bits
    me = lax.axis_index("dom")
    bit = [lax.rem(lax.div(me, 1 << s), 2) for s in range(steps)]
    partner = [me + (1 - 2 * bit[s]) * (1 << s) for s in range(steps)]
    if last:
        keep_own = bit[bits] == lax.axis_index("band")

    barrier = pltpu.get_barrier_semaphore()
    for s in range(steps):
        pl.semaphore_signal(barrier, inc=1, device_id={"dom": partner[s]}, device_id_type=pl.DeviceIdType.MESH)
    pl.semaphore_wait(barrier, steps)

    def source(s):
        return tile if s == 0 else sums[s - 1]

    def copy(s, c):
        cols = pl.ds(c * chunk, chunk)
        if s < bits:
            half = blocks >> (s + 1)
            src = source(s).at[pl.ds((1 - bit[s]) * half, half), :, cols]
            dst = came[s].at[:, :, cols]
        else:
            src, dst = leaving.at[:, cols], arrived.at[:, cols]
        return pltpu.make_async_remote_copy(
            src_ref=src, dst_ref=dst, send_sem=send_sem.at[s, c], recv_sem=recv_sem.at[s, c],
            device_id={"dom": partner[s]}, device_id_type=pl.DeviceIdType.MESH,
        )

    started = {}

    def send(s, c):
        started[s, c] = copy(s, c)
        started[s, c].start()

    for c in range(chunks):
        send(0, c)
    for turn in range(chunks + steps - 1):
        for s in reversed(range(steps)):
            c = turn - s
            if not 0 <= c < chunks:
                continue
            cols = pl.ds(c * chunk, chunk)
            started[s, c].wait_recv()
            if s < bits:
                half = blocks >> (s + 1)
                total = source(s)[pl.ds(bit[s] * half, half), :, cols] + came[s][:, :, cols]
                sums[s][:, :, cols] = total
                if s < bits - 1:
                    send(s + 1, c)
                elif last:
                    mine = own[:, cols]
                    leaving[:, cols] = jnp.where(keep_own, total[0], mine)
                    out[:, cols] = jnp.where(keep_own, mine, total[0])
                    send(bits, c)
                else:
                    out[:, cols] = total[0]
            else:
                out[:, cols] = out[:, cols] + arrived[:, cols]
    for one in started.values():
        one.wait_send()


def halving(tile, own, blocks):
    bits = blocks.bit_length() - 1
    rows, width = tile.shape[1:]
    last = own is not None
    chunk = 256
    scratch = [pltpu.VMEM((blocks >> (s + 1), rows, width), jnp.float32) for s in range(bits)] * 2
    if last:
        scratch += [pltpu.VMEM((rows, width), jnp.float32)] * 2
    sems = pltpu.SemaphoreType.DMA((bits + 1, width // chunk))
    operands = (tile, own) if last else (tile,)
    return pl.pallas_call(
        functools.partial(halving_kernel, blocks, chunk, last),
        out_shape=jax.ShapeDtypeStruct((rows, width), jnp.float32),
        in_specs=[pl.BlockSpec(memory_space=pltpu.VMEM)] * len(operands),
        out_specs=pl.BlockSpec(memory_space=pltpu.VMEM),
        scratch_shapes=scratch + [sems, sems],
        compiler_params=pltpu.CompilerParams(
            collective_id=1 if last else 0, has_side_effects=True, vmem_limit_bytes=32 * 2**20
        ),
        cost_estimate=pl.CostEstimate(flops=0, bytes_accessed=64 * 2**20, transcendentals=0),
    )(*operands)


def on_device(wavefunctions, cell_hamiltonian, face_nodes):
    cells, nodes, width = wavefunctions.shape
    faces = face_nodes[0]
    slots = faces.reshape(-1)
    owner = slots // nodes
    rows = cell_hamiltonian.reshape(cells * nodes, nodes)[slots]
    mine = owner[None, :] == jnp.arange(cells)[:, None]
    rim_ham = jnp.where(mine[:, :, None], rows[None], 0.0)
    rim_ham = jnp.swapaxes(rim_ham, 0, 1).reshape(slots.shape[0], cells * nodes)
    spread = (jnp.arange(cells * nodes)[:, None] == slots[None, :]).astype(jnp.float32)

    def assembled(field):
        flat = field.reshape(cells * nodes, width)
        rims = jnp.dot(rim_ham, flat, precision=HIGH, preferred_element_type=jnp.float32)
        rims = rims.reshape(2, faces.shape[1], width)
        lower = passed_along(rims[1], "dom", 1)
        upper = passed_along(rims[0], "dom", -1)
        local = local_step(field, cell_hamiltonian)
        came = jnp.concatenate([lower, upper], axis=0)
        gained = jnp.dot(spread, came, precision=HIGH, preferred_element_type=jnp.float32)
        return local + gained.reshape(field.shape)

    previous = wavefunctions
    current = 0.5 * assembled(wavefunctions)
    for step in range(DEGREE - 1):
        following = assembled(current) - previous
        previous = current
        current = following
    flat = current.reshape(cells * nodes, width)
    other = passed_along(flat, "band", 1)

    def inner_block(left, right):
        return lax.dot_general(
            left, right, (((0,), (0,)), ((), ())), precision=HIGH, preferred_element_type=jnp.float32
        )

    count = lax.axis_size("dom")
    blocks = count // 2
    own_tile = inner_block(flat, flat)
    own_sum = halving(by_bits(own_tile, blocks), None, blocks)
    cross_tile = inner_block(other, flat)
    margin = halving(by_bits(cross_tile, blocks), own_sum, blocks)
    margin = margin / float(CELL_DEV * NODES)
    return (current, margin)


def solution(mesh):
    return jax.shard_map(
        on_device,
        mesh=mesh,
        in_specs=(P("dom", None, "band"), P("dom", None, None), P("dom", None, None)),
        out_specs=(P("dom", None, "band"), P("dom", "band")),
        check_vma=False,
    )
```

```python
import functools

import jax
import jax.numpy as jnp
from jax import lax
from jax.experimental import pallas as pl
from jax.experimental.pallas import tpu as pltpu
from jax.sharding import PartitionSpec as P

NODES = 512
CELL_DEV = 2
DEGREE = 4
HIGH = lax.Precision.HIGH


def passed_along(value, axis, steps):
    count = lax.axis_size(axis)
    pairs = [(source, (source + steps) % count) for source in range(count)]
    return lax.ppermute(value, axis, pairs)


def local_step(field, ham):
    return lax.dot_general(
        ham, field, (((2,), (1,)), ((0,), (0,))), precision=HIGH, preferred_element_type=jnp.float32
    )


def by_bits(tile, blocks):
    bits = blocks.bit_length() - 1
    rows, width = tile.shape[0] // blocks, tile.shape[1]
    cut = tile.reshape((2,) * bits + (rows, width))
    order = tuple(reversed(range(bits))) + (bits, bits + 1)
    return jnp.transpose(cut, order).reshape(blocks, rows, width)


def halving_kernel(blocks, chunk, last, *refs):
    bits = blocks.bit_length() - 1
    refs = list(refs)
    tile = refs.pop(0)
    own = refs.pop(0) if last else None
    out = refs.pop(0)
    sums = [refs.pop(0) for _ in range(bits)]
    came = [refs.pop(0) for _ in range(bits)]
    if last:
        leaving, arrived = refs.pop(0), refs.pop(0)
    send_sem, recv_sem = refs
    chunks = tile.shape[2] // chunk
    steps = bits + 1 if last else bits
    me = lax.axis_index("dom")
    bit = [lax.rem(lax.div(me, 1 << s), 2) for s in range(steps)]
    partner = [me + (1 - 2 * bit[s]) * (1 << s) for s in range(steps)]
    if last:
        keep_own = bit[bits] == lax.axis_index("band")

    barrier = pltpu.get_barrier_semaphore()
    for s in range(steps):
        pl.semaphore_signal(barrier, inc=1, device_id={"dom": partner[s]}, device_id_type=pl.DeviceIdType.MESH)
    pl.semaphore_wait(barrier, steps)

    def source(s):
        return tile if s == 0 else sums[s - 1]

    def copy(s, c):
        cols = pl.ds(c * chunk, chunk)
        if s < bits:
            half = blocks >> (s + 1)
            src = source(s).at[pl.ds((1 - bit[s]) * half, half), :, cols]
            dst = came[s].at[:, :, cols]
        else:
            src, dst = leaving.at[:, cols], arrived.at[:, cols]
        return pltpu.make_async_remote_copy(
            src_ref=src, dst_ref=dst, send_sem=send_sem.at[s, c], recv_sem=recv_sem.at[s, c],
            device_id={"dom": partner[s]}, device_id_type=pl.DeviceIdType.MESH,
        )

    started = {}

    def send(s, c):
        started[s, c] = copy(s, c)
        started[s, c].start()

    for c in range(chunks):
        send(0, c)
    for turn in range(chunks + steps - 1):
        for s in reversed(range(steps)):
            c = turn - s
            if not 0 <= c < chunks:
                continue
            cols = pl.ds(c * chunk, chunk)
            started[s, c].wait_recv()
            if s < bits:
                half = blocks >> (s + 1)
                total = source(s)[pl.ds(bit[s] * half, half), :, cols] + came[s][:, :, cols]
                sums[s][:, :, cols] = total
                if s < bits - 1:
                    send(s + 1, c)
                elif last:
                    mine = own[:, cols]
                    leaving[:, cols] = jnp.where(keep_own, total[0], mine)
                    out[:, cols] = jnp.where(keep_own, mine, total[0])
                    send(bits, c)
                else:
                    out[:, cols] = total[0]
            else:
                out[:, cols] = out[:, cols] + arrived[:, cols]
    for one in started.values():
        one.wait_send()


def halving(tile, own, blocks, number):
    bits = blocks.bit_length() - 1
    rows, width = tile.shape[1:]
    last = own is not None
    chunk = 256
    scratch = [pltpu.VMEM((blocks >> (s + 1), rows, width), jnp.float32) for s in range(bits)] * 2
    if last:
        scratch += [pltpu.VMEM((rows, width), jnp.float32)] * 2
    sems = pltpu.SemaphoreType.DMA((bits + 1, width // chunk))
    operands = (tile, own) if last else (tile,)
    return pl.pallas_call(
        functools.partial(halving_kernel, blocks, chunk, last),
        out_shape=jax.ShapeDtypeStruct((rows, width), jnp.float32),
        in_specs=[pl.BlockSpec(memory_space=pltpu.VMEM)] * len(operands),
        out_specs=pl.BlockSpec(memory_space=pltpu.VMEM),
        scratch_shapes=scratch + [sems, sems],
        compiler_params=pltpu.CompilerParams(
            collective_id=number, has_side_effects=True, vmem_limit_bytes=32 * 2**20
        ),
        cost_estimate=pl.CostEstimate(flops=0, bytes_accessed=64 * 2**20, transcendentals=0),
    )(*operands)


def on_device(wavefunctions, cell_hamiltonian, face_nodes):
    cells, nodes, width = wavefunctions.shape
    faces = face_nodes[0]
    slots = faces.reshape(-1)
    owner = slots // nodes
    rows = cell_hamiltonian.reshape(cells * nodes, nodes)[slots]
    mine = owner[None, :] == jnp.arange(cells)[:, None]
    rim_ham = jnp.where(mine[:, :, None], rows[None], 0.0)
    rim_ham = jnp.swapaxes(rim_ham, 0, 1).reshape(slots.shape[0], cells * nodes)
    spread = (jnp.arange(cells * nodes)[:, None] == slots[None, :]).astype(jnp.float32)

    def assembled(field):
        flat = field.reshape(cells * nodes, width)
        rims = jnp.dot(rim_ham, flat, precision=HIGH, preferred_element_type=jnp.float32)
        rims = rims.reshape(2, faces.shape[1], width)
        lower = passed_along(rims[1], "dom", 1)
        upper = passed_along(rims[0], "dom", -1)
        local = local_step(field, cell_hamiltonian)
        came = jnp.concatenate([lower, upper], axis=0)
        gained = jnp.dot(spread, came, precision=HIGH, preferred_element_type=jnp.float32)
        return local + gained.reshape(field.shape)

    previous = wavefunctions
    current = 0.5 * assembled(wavefunctions)
    for step in range(DEGREE - 1):
        following = assembled(current) - previous
        previous = current
        current = following
    flat = current.reshape(cells * nodes, width)

    def rows_of(left):
        return jnp.dot(left, flat, precision=HIGH, preferred_element_type=jnp.float32)

    blocks = lax.axis_size("dom") // 2
    turned = by_bits(flat.T, blocks)
    own_tile = rows_of(turned.reshape(width, -1)).reshape(blocks, -1, width)
    half = turned.shape[1] // 2
    first, second = turned[:, :half].reshape(blocks * half, -1), turned[:, half:].reshape(blocks * half, -1)
    other = passed_along(first, "band", 1)
    own_sum = halving(own_tile, None, blocks, 0)
    second, other, own_sum = lax.optimization_barrier((second, other, own_sum))
    later = passed_along(second, "band", 1)
    upper = halving(rows_of(other).reshape(blocks, half, width), own_sum[:half], blocks, 1)
    later, upper = lax.optimization_barrier((later, upper))
    lower = halving(rows_of(later).reshape(blocks, half, width), own_sum[half:], blocks, 2)
    margin = jnp.concatenate([upper, lower], axis=0)
    margin = margin / float(CELL_DEV * NODES)
    return (current, margin)


def solution(mesh):
    return jax.shard_map(
        on_device,
        mesh=mesh,
        in_specs=(P("dom", None, "band"), P("dom", None, None), P("dom", None, None)),
        out_specs=(P("dom", None, "band"), P("dom", "band")),
        check_vma=False,
    )
```

```python
import functools

import jax
import jax.numpy as jnp
from jax import lax
from jax.experimental import pallas as pl
from jax.experimental.pallas import tpu as pltpu
from jax.sharding import PartitionSpec as P

NODES = 512
CELL_DEV = 2
DEGREE = 4
HIGH = lax.Precision.HIGH


def passed_along(value, axis, steps):
    count = lax.axis_size(axis)
    pairs = [(source, (source + steps) % count) for source in range(count)]
    return lax.ppermute(value, axis, pairs)


def local_step(field, ham):
    return lax.dot_general(
        ham, field, (((2,), (1,)), ((0,), (0,))), precision=HIGH, preferred_element_type=jnp.float32
    )


def by_bits(tile, blocks):
    bits = blocks.bit_length() - 1
    rows, width = tile.shape[0] // blocks, tile.shape[1]
    cut = tile.reshape((2,) * bits + (rows, width))
    order = tuple(reversed(range(bits))) + (bits, bits + 1)
    return jnp.transpose(cut, order).reshape(blocks, rows, width)


def halving_kernel(blocks, chunk, last, *refs):
    bits = blocks.bit_length() - 1
    refs = list(refs)
    tile = refs.pop(0)
    own = refs.pop(0) if last else None
    out = refs.pop(0)
    sums = [refs.pop(0) for _ in range(bits)]
    came = [refs.pop(0) for _ in range(bits)]
    if last:
        leaving, arrived = refs.pop(0), refs.pop(0)
    send_sem, recv_sem = refs
    chunks = tile.shape[2] // chunk
    steps = bits + 1 if last else bits
    me = lax.axis_index("dom")
    bit = [lax.rem(lax.div(me, 1 << s), 2) for s in range(steps)]
    partner = [me + (1 - 2 * bit[s]) * (1 << s) for s in range(steps)]
    if last:
        keep_own = bit[bits] == lax.axis_index("band")

    barrier = pltpu.get_barrier_semaphore()
    for s in range(steps):
        pl.semaphore_signal(barrier, inc=1, device_id={"dom": partner[s]}, device_id_type=pl.DeviceIdType.MESH)
    pl.semaphore_wait(barrier, steps)

    def source(s):
        return tile if s == 0 else sums[s - 1]

    def copy(s, c):
        cols = pl.ds(c * chunk, chunk)
        if s < bits:
            half = blocks >> (s + 1)
            src = source(s).at[pl.ds((1 - bit[s]) * half, half), :, cols]
            dst = came[s].at[:, :, cols]
        else:
            src, dst = leaving.at[:, cols], arrived.at[:, cols]
        return pltpu.make_async_remote_copy(
            src_ref=src, dst_ref=dst, send_sem=send_sem.at[s, c], recv_sem=recv_sem.at[s, c],
            device_id={"dom": partner[s]}, device_id_type=pl.DeviceIdType.MESH,
        )

    started = {}

    def send(s, c):
        started[s, c] = copy(s, c)
        started[s, c].start()

    for c in range(chunks):
        send(0, c)
    order = [(0, c) for c in range(chunks)]
    for turn in range(chunks + bits - 2):
        order += [(s, turn - s + 1) for s in range(1, bits) if 0 <= turn - s + 1 < chunks]
    if last:
        order += [(bits, c) for c in range(chunks)]
    for s, c in order:
        cols = pl.ds(c * chunk, chunk)
        started[s, c].wait_recv()
        if s < bits:
            half = blocks >> (s + 1)
            total = source(s)[pl.ds(bit[s] * half, half), :, cols] + came[s][:, :, cols]
            sums[s][:, :, cols] = total
            if s < bits - 1:
                send(s + 1, c)
            elif last:
                mine = own[:, cols]
                leaving[:, cols] = jnp.where(keep_own, total[0], mine)
                out[:, cols] = jnp.where(keep_own, mine, total[0])
                send(bits, c)
            else:
                out[:, cols] = total[0]
        else:
            out[:, cols] = out[:, cols] + arrived[:, cols]
    for one in started.values():
        one.wait_send()


def halving(tile, own, blocks, number):
    bits = blocks.bit_length() - 1
    rows, width = tile.shape[1:]
    last = own is not None
    chunk = 256
    scratch = [pltpu.VMEM((blocks >> (s + 1), rows, width), jnp.float32) for s in range(bits)] * 2
    if last:
        scratch += [pltpu.VMEM((rows, width), jnp.float32)] * 2
    sems = pltpu.SemaphoreType.DMA((bits + 1, width // chunk))
    operands = (tile, own) if last else (tile,)
    return pl.pallas_call(
        functools.partial(halving_kernel, blocks, chunk, last),
        out_shape=jax.ShapeDtypeStruct((rows, width), jnp.float32),
        in_specs=[pl.BlockSpec(memory_space=pltpu.VMEM)] * len(operands),
        out_specs=pl.BlockSpec(memory_space=pltpu.VMEM),
        scratch_shapes=scratch + [sems, sems],
        compiler_params=pltpu.CompilerParams(
            collective_id=number, has_side_effects=True, vmem_limit_bytes=32 * 2**20
        ),
        cost_estimate=pl.CostEstimate(flops=0, bytes_accessed=64 * 2**20, transcendentals=0),
    )(*operands)


def on_device(wavefunctions, cell_hamiltonian, face_nodes):
    cells, nodes, width = wavefunctions.shape
    faces = face_nodes[0]
    slots = faces.reshape(-1)
    owner = slots // nodes
    rows = cell_hamiltonian.reshape(cells * nodes, nodes)[slots]
    mine = owner[None, :] == jnp.arange(cells)[:, None]
    rim_ham = jnp.where(mine[:, :, None], rows[None], 0.0)
    rim_ham = jnp.swapaxes(rim_ham, 0, 1).reshape(slots.shape[0], cells * nodes)
    spread = (jnp.arange(cells * nodes)[:, None] == slots[None, :]).astype(jnp.float32)

    def assembled(field):
        flat = field.reshape(cells * nodes, width)
        rims = jnp.dot(rim_ham, flat, precision=HIGH, preferred_element_type=jnp.float32)
        rims = rims.reshape(2, faces.shape[1], width)
        lower = passed_along(rims[1], "dom", 1)
        upper = passed_along(rims[0], "dom", -1)
        local = local_step(field, cell_hamiltonian)
        came = jnp.concatenate([lower, upper], axis=0)
        gained = jnp.dot(spread, came, precision=HIGH, preferred_element_type=jnp.float32)
        return local + gained.reshape(field.shape)

    previous = wavefunctions
    current = 0.5 * assembled(wavefunctions)
    for step in range(DEGREE - 1):
        following = assembled(current) - previous
        previous = current
        current = following
    flat = current.reshape(cells * nodes, width)

    def rows_of(left):
        return jnp.dot(left, flat, precision=HIGH, preferred_element_type=jnp.float32)

    blocks = lax.axis_size("dom") // 2
    turned = by_bits(flat.T, blocks)
    own_tile = rows_of(turned.reshape(width, -1)).reshape(blocks, -1, width)
    half = turned.shape[1] // 2
    first, second = turned[:, :half].reshape(blocks * half, -1), turned[:, half:].reshape(blocks * half, -1)
    other = passed_along(first, "band", 1)
    own_sum = halving(own_tile, None, blocks, 0)
    second, other, own_sum = lax.optimization_barrier((second, other, own_sum))
    later = passed_along(second, "band", 1)
    upper = halving(rows_of(other).reshape(blocks, half, width), own_sum[:half], blocks, 1)
    later, upper = lax.optimization_barrier((later, upper))
    lower = halving(rows_of(later).reshape(blocks, half, width), own_sum[half:], blocks, 2)
    margin = jnp.concatenate([upper, lower], axis=0)
    margin = margin / float(CELL_DEV * NODES)
    return (current, margin)


def solution(mesh):
    return jax.shard_map(
        on_device,
        mesh=mesh,
        in_specs=(P("dom", None, "band"), P("dom", None, None), P("dom", None, None)),
        out_specs=(P("dom", None, "band"), P("dom", "band")),
        check_vma=False,
    )
```

```python
import functools

import jax
import jax.numpy as jnp
from jax import lax
from jax.experimental import pallas as pl
from jax.experimental.pallas import tpu as pltpu
from jax.sharding import PartitionSpec as P

NODES = 512
CELL_DEV = 2
DEGREE = 4
HIGH = lax.Precision.HIGH


def passed_along(value, axis, steps):
    count = lax.axis_size(axis)
    pairs = [(source, (source + steps) % count) for source in range(count)]
    return lax.ppermute(value, axis, pairs)


def local_step(field, ham):
    return lax.dot_general(
        ham, field, (((2,), (1,)), ((0,), (0,))), precision=HIGH, preferred_element_type=jnp.float32
    )


def by_bits(tile, blocks):
    bits = blocks.bit_length() - 1
    rows, width = tile.shape[0] // blocks, tile.shape[1]
    cut = tile.reshape((2,) * bits + (rows, width))
    order = tuple(reversed(range(bits))) + (bits, bits + 1)
    return jnp.transpose(cut, order).reshape(blocks, rows, width)


def halving_kernel(blocks, chunk, last, *refs):
    bits = blocks.bit_length() - 1
    refs = list(refs)
    tile = refs.pop(0)
    own = refs.pop(0) if last else None
    out = refs.pop(0)
    sums = [refs.pop(0) for _ in range(bits)]
    came = [refs.pop(0) for _ in range(bits)]
    if last:
        leaving, arrived = refs.pop(0), refs.pop(0)
    send_sem, recv_sem = refs
    chunks = tile.shape[2] // chunk
    steps = bits + 1 if last else bits
    me = lax.axis_index("dom")
    bit = [lax.rem(lax.div(me, 1 << s), 2) for s in range(steps)]
    partner = [me + (1 - 2 * bit[s]) * (1 << s) for s in range(steps)]
    if last:
        keep_own = bit[bits] == lax.axis_index("band")

    barrier = pltpu.get_barrier_semaphore()
    for s in range(steps):
        pl.semaphore_signal(barrier, inc=1, device_id={"dom": partner[s]}, device_id_type=pl.DeviceIdType.MESH)
    pl.semaphore_wait(barrier, steps)

    def source(s):
        return tile if s == 0 else sums[s - 1]

    def copy(s, c):
        cols = pl.ds(c * chunk, chunk)
        if s < bits:
            half = blocks >> (s + 1)
            src = source(s).at[pl.ds((1 - bit[s]) * half, half), :, cols]
            dst = came[s].at[:, :, cols]
        else:
            src, dst = leaving.at[:, cols], arrived.at[:, cols]
        return pltpu.make_async_remote_copy(
            src_ref=src, dst_ref=dst, send_sem=send_sem.at[s, c], recv_sem=recv_sem.at[s, c],
            device_id={"dom": partner[s]}, device_id_type=pl.DeviceIdType.MESH,
        )

    started = {}

    def send(s, c):
        started[s, c] = copy(s, c)
        started[s, c].start()

    for c in range(chunks):
        send(0, c)
    order = [(0, c) for c in range(chunks)]
    for turn in range(chunks + bits - 2):
        order += [(s, turn - s + 1) for s in range(1, bits) if 0 <= turn - s + 1 < chunks]
    if last:
        order += [(bits, c) for c in range(chunks)]
    for s, c in order:
        cols = pl.ds(c * chunk, chunk)
        started[s, c].wait_recv()
        if s < bits:
            half = blocks >> (s + 1)
            total = source(s)[pl.ds(bit[s] * half, half), :, cols] + came[s][:, :, cols]
            sums[s][:, :, cols] = total
            if s < bits - 1:
                send(s + 1, c)
            elif last:
                mine = own[:, cols]
                leaving[:, cols] = jnp.where(keep_own, total[0], mine)
                out[:, cols] = jnp.where(keep_own, mine, total[0])
                send(bits, c)
            else:
                out[:, cols] = total[0]
        else:
            out[:, cols] = out[:, cols] + arrived[:, cols]
    for one in started.values():
        one.wait_send()


def halving(tile, own, blocks, number):
    bits = blocks.bit_length() - 1
    rows, width = tile.shape[1:]
    last = own is not None
    chunk = 256
    scratch = [pltpu.VMEM((blocks >> (s + 1), rows, width), jnp.float32) for s in range(bits)] * 2
    if last:
        scratch += [pltpu.VMEM((rows, width), jnp.float32)] * 2
    sems = pltpu.SemaphoreType.DMA((bits + 1, width // chunk))
    operands = (tile, own) if last else (tile,)
    return pl.pallas_call(
        functools.partial(halving_kernel, blocks, chunk, last),
        out_shape=jax.ShapeDtypeStruct((rows, width), jnp.float32),
        in_specs=[pl.BlockSpec(memory_space=pltpu.VMEM)] * len(operands),
        out_specs=pl.BlockSpec(memory_space=pltpu.VMEM),
        scratch_shapes=scratch + [sems, sems],
        compiler_params=pltpu.CompilerParams(
            collective_id=number, has_side_effects=True, vmem_limit_bytes=32 * 2**20
        ),
        cost_estimate=pl.CostEstimate(flops=0, bytes_accessed=64 * 2**20, transcendentals=0),
    )(*operands)


def on_device(wavefunctions, cell_hamiltonian, face_nodes):
    cells, nodes, width = wavefunctions.shape
    faces = face_nodes[0]
    slots = faces.reshape(-1)
    owner = slots // nodes
    rows = cell_hamiltonian.reshape(cells * nodes, nodes)[slots]
    mine = owner[None, :] == jnp.arange(cells)[:, None]
    rim_ham = jnp.where(mine[:, :, None], rows[None], 0.0)
    rim_ham = jnp.swapaxes(rim_ham, 0, 1).reshape(slots.shape[0], cells * nodes)
    spread = (jnp.arange(cells * nodes)[:, None] == slots[None, :]).astype(jnp.float32)

    def assembled(field):
        flat = field.reshape(cells * nodes, width)
        rims = jnp.dot(rim_ham, flat, precision=HIGH, preferred_element_type=jnp.float32)
        rims = rims.reshape(2, faces.shape[1], width)
        lower = passed_along(rims[1], "dom", 1)
        upper = passed_along(rims[0], "dom", -1)
        local = local_step(field, cell_hamiltonian)
        came = jnp.concatenate([lower, upper], axis=0)
        gained = jnp.dot(spread, came, precision=HIGH, preferred_element_type=jnp.float32)
        return local + gained.reshape(field.shape)

    previous = wavefunctions
    current = 0.5 * assembled(wavefunctions)
    for step in range(DEGREE - 1):
        following = assembled(current) - previous
        previous = current
        current = following
    flat = current.reshape(cells * nodes, width)

    def rows_of(left):
        return jnp.dot(left, flat, precision=HIGH, preferred_element_type=jnp.float32)

    blocks = lax.axis_size("dom") // 2
    turned = by_bits(flat.T, blocks)
    own_tile = rows_of(turned.reshape(width, -1)).reshape(blocks, -1, width)
    rows = turned.shape[1]
    half = 2 * rows // 3
    first, second = turned[:, :half].reshape(blocks * half, -1), turned[:, half:].reshape(blocks * (rows - half), -1)
    other = passed_along(first, "band", 1)
    own_sum = halving(own_tile, None, blocks, 0)
    second, other, own_sum = lax.optimization_barrier((second, other, own_sum))
    later = passed_along(second, "band", 1)
    upper = halving(rows_of(other).reshape(blocks, half, width), own_sum[:half], blocks, 1)
    later, upper = lax.optimization_barrier((later, upper))
    lower = halving(rows_of(later).reshape(blocks, rows - half, width), own_sum[half:], blocks, 2)
    margin = jnp.concatenate([upper, lower], axis=0)
    margin = margin / float(CELL_DEV * NODES)
    return (current, margin)


def solution(mesh):
    return jax.shard_map(
        on_device,
        mesh=mesh,
        in_specs=(P("dom", None, "band"), P("dom", None, None), P("dom", None, None)),
        out_specs=(P("dom", None, "band"), P("dom", "band")),
        check_vma=False,
    )
```
